512 devices in a mesh: seq: 32 (over x_hi, y, core), batch: 16 (over z, x_lo).
Axes of the slice: x: 4 (x_hi: 2, x_lo: 2; x = x_hi * 2 + x_lo), y: 8, z: 8, core: 2. Of those that a mesh axis runs over, the one named last changes fastest.
Arguments:
- inputs: bfloat16 [16, 32768, 512], P('batch', 'seq'), may hold values from -6 to 6
- gates: bfloat16 [16, 32768, 512], P('batch', 'seq'), may hold values from 0.099609375 to 2
- cotangent: bfloat16 [16, 32768, 512], P('batch', 'seq'), may hold values from -6 to 6
- first_factor: bfloat16 [128, 256, 256], P('seq'), may hold values from -0.375 to 0.375
- second_factor: bfloat16 [256, 128, 128], P('seq'), may hold values from -0.5 to 0.5
Outputs:
- input_grad: bfloat16 [16, 32768, 512], P('batch', 'seq')
- first_grad: float32 [128, 256, 256], P('seq', 'batch')
- second_grad: float32 [256, 128, 128], P('seq', 'batch')
The draws below stay inside these ranges and needn't reach their ends.
All inputs are finite; a program needn't handle non-finite values.
Results may differ from the reference program's by a relative error of at most 0.0057.
Values may be sent and summed in bfloat16 or wider, within the bound.
No kernel may reach another device: no remote copies, remote signals or barrier semaphores. Data moves between devices by JAX's collectives and lax.ppermute only.
A program may use at most 64 MiB of HBM per device.

```python
import math
import jax
import jax.numpy as jnp
from jax import lax

P_SIZE = 128
Q = 256
C = 512
L = 32768
SEQS = 16


def shard_levels(rng, shape, split, least, largest):
    gain = 1.0
    for axis_at, shards_of in split:
        heights = jax.random.uniform(jax.random.fold_in(jax.random.fold_in(rng, 6), axis_at), (shards_of,), jnp.float32, least / len(split), largest / len(split))
        gain = gain * jnp.repeat(jnp.exp(heights), shape[axis_at] // shards_of).reshape((-1,) + (1,) * (len(shape) - 1 - axis_at))
    return gain


def bell_draw(own_key, shape, width, most, cuts=(), dtype=jnp.bfloat16):
    result = width * jax.random.normal(own_key, shape, jnp.float32)
    if cuts:
        result = result * shard_levels(own_key, shape, cuts, -0.22, 0.18)
    return jnp.clip(result, -most, most).astype(dtype)


def setup_inputs(seed: int = 0) -> dict:
    key_list = jax.random.split(jax.random.key(seed), 6)
    inputs = bell_draw(key_list[0], (SEQS, L, C), 1.0, 6.0, ((0, 16), (1, 32)))
    gates = jnp.clip(jnp.exp(math.log(2.0) - 2.9996462 * jax.random.uniform(key_list[1], (SEQS, L, C), jnp.float32) ** shard_levels(key_list[1], (SEQS, L, C), ((0, 16), (1, 32)), -0.2, 0.2)), 0.099609375, 2.0).astype(jnp.bfloat16)
    cotangent = bell_draw(key_list[2], (SEQS, L, C), 1.0, 6.0, ((0, 16), (1, 32)))
    first_factor = bell_draw(key_list[3], (P_SIZE, Q, Q), Q ** -0.5, 0.375, ((0, 32),))
    second_factor = bell_draw(key_list[4], (Q, P_SIZE, P_SIZE), P_SIZE ** -0.5, 0.5, ((0, 32),))
    return dict(inputs=inputs, gates=gates, cotangent=cotangent, first_factor=first_factor, second_factor=second_factor)


def reference(inputs, gates, cotangent, first_factor, second_factor):
    first_wide = first_factor.astype(jnp.float32)
    second_wide = second_factor.astype(jnp.float32)

    def step(carry, item):
        first_acc, second_acc = carry
        seq_input, seq_gate, seq_cot = item
        source = seq_input.reshape(P_SIZE, Q, C).astype(jnp.float32)
        mixed = jnp.einsum("pij,pjc->pic", first_wide, source).astype(jnp.bfloat16)
        spread = jnp.transpose(mixed, (1, 0, 2)).astype(jnp.float32)
        scaled = (seq_cot.astype(jnp.float32) * seq_gate.astype(jnp.float32)).astype(jnp.bfloat16)
        scaled = scaled.reshape(Q, P_SIZE, C).astype(jnp.float32)
        second_acc = second_acc + jnp.einsum("qkc,qpc->qkp", scaled, spread)
        back = jnp.einsum("qkp,qkc->qpc", second_wide, scaled).astype(jnp.bfloat16)
        returned = jnp.transpose(back, (1, 0, 2)).astype(jnp.float32)
        grad = jnp.einsum("pij,pic->pjc", first_wide, returned).astype(jnp.bfloat16)
        first_acc = first_acc + jnp.einsum("pic,pjc->pij", returned, source)
        return (first_acc, second_acc), grad.reshape(P_SIZE * Q, C)

    start = (jnp.zeros((P_SIZE, Q, Q), jnp.float32), jnp.zeros((Q, P_SIZE, P_SIZE), jnp.float32))
    (first_acc, second_acc), grads = lax.scan(step, start, (inputs, gates, cotangent))
    total = inputs.shape[0]
    return grads, first_acc / total, second_acc / total
```

```python
import jax
import jax.numpy as jnp
from jax import lax
from jax.experimental import pallas as pl
from jax.experimental.pallas import tpu as pltpu
from jax.sharding import PartitionSpec as P

F32 = jnp.float32
BF16 = jnp.bfloat16
CHUNK = 256
LANES = 128
MIB = 1024 * 1024


def dot(a, b, contract_a, contract_b):
    return lax.dot_general(a, b, (((contract_a,), (contract_b,)), ((), ())), preferred_element_type=F32)


def product(cotangent, gates):
    return (cotangent.astype(F32) * gates.astype(F32)).astype(BF16)


def send_kernel(inputs, gates, cotangent, first, second, send, spread):
    rows, width_p, _ = second.shape
    blocks, width_q, _ = first.shape
    owners, lines, chunk = send.shape
    lines //= 2
    for q in range(rows):
        part = pl.ds(q * width_p, width_p)
        back = dot(second[q], product(cotangent[0, part, :], gates[0, part, :]), 0, 0)
        for lane in range(spread.shape[0]):
            spread[lane, pl.ds(q, width_p, stride=rows), :] = back[:, lane * LANES:(lane + 1) * LANES]
    for lane in range(spread.shape[0]):
        send[:, :lines, lane * LANES:(lane + 1) * LANES] = (
            spread[lane].reshape(owners, lines, LANES).astype(BF16)
        )
    parts = []
    for p in range(blocks):
        mixed = dot(first[p], inputs[0, p * width_q:(p + 1) * width_q, :], 1, 0)
        parts.append(mixed.reshape(owners, rows, chunk))
    send[:, lines:, :] = jnp.concatenate(parts, axis=1).astype(BF16)


def grads_kernel(got, inputs, gates, cotangent, out, spread):
    owners, lines, channels = got.shape
    lines //= 2
    shares, height, width_q = out.shape
    width_p = LANES
    rows = gates.shape[1] // width_p
    blocks = inputs.shape[1] // width_q
    wide = got[:, :lines, :].astype(F32).reshape(owners, blocks, rows, channels)
    parts = []
    for p in range(blocks):
        back = wide[:, p].reshape(width_q, channels).astype(BF16)
        grad = dot(back, inputs[0, p * width_q:(p + 1) * width_q, :], 1, 1)
        parts.append(grad.reshape(shares, width_q // shares, width_q))
    for lane in range(spread.shape[0]):
        spread[lane] = (
            got[:, lines:, lane * LANES:(lane + 1) * LANES].astype(F32).reshape(owners * lines, LANES)
        )
    seconds = []
    for q in range(rows):
        mixed = jnp.concatenate(
            [spread[lane, pl.ds(q, width_p, stride=rows), :] for lane in range(spread.shape[0])], axis=1
        ).astype(BF16)
        part = pl.ds(q * width_p, width_p)
        grad = dot(product(cotangent[0, part, :], gates[0, part, :]), mixed, 1, 1)
        seconds.append(grad.reshape(shares, width_p // shares, width_p))
    half = rows // 2
    for q in range(half):
        parts.append(jnp.concatenate([seconds[q], seconds[q + half]], axis=2))
    out[...] = jnp.concatenate(parts, axis=1).astype(BF16)


def input_kernel(got, factor, out):
    blocks, width, _ = factor.shape
    owners, lines, channels = got.shape
    wide = got[:, :lines // 2, :].astype(F32).reshape(owners, blocks, width // owners, channels)
    for p in range(blocks):
        back = wide[:, p].reshape(width, channels).astype(BF16)
        out[0, p * width:(p + 1) * width, :] = dot(factor[p], back, 0, 0).astype(BF16)


def sum_kernel(got, first, second):
    shares = got.shape[0]
    blocks, height, width_q = first.shape
    rows, depth, width_p = second.shape
    total = got[0].astype(F32)
    for share in range(1, shares):
        total = total + got[share].astype(F32)
    total = total * (1.0 / shares)
    cut = blocks * height
    first[...] = total[:cut].reshape(first.shape)
    half = rows // 2
    second[:half] = total[cut:, :width_p].reshape(half, depth, width_p)
    second[half:] = total[cut:, width_p:].reshape(half, depth, width_p)


def whole(shape):
    return pl.BlockSpec(shape, lambda i: (0,) * len(shape))


def sliced(shape):
    return pl.BlockSpec(shape[:-1] + (CHUNK,), lambda i: (0,) * (len(shape) - 1) + (i,))


def near(count):
    return [pl.BlockSpec(memory_space=pltpu.VMEM)] * count


def cost(flops, bytes_accessed):
    return pl.CostEstimate(flops=flops, bytes_accessed=bytes_accessed, transcendentals=0)


def per_device(inputs, gates, cotangent, first_factor, second_factor):
    _, positions, channels = inputs.shape
    blocks, width_q, _ = first_factor.shape
    rows, width_p, _ = second_factor.shape
    owners = lax.axis_size("seq")
    shares = lax.axis_size("batch")
    packet = (owners, 2 * blocks * rows, channels)
    macs = positions * channels

    send = pl.pallas_call(
        send_kernel,
        grid=(channels // CHUNK,),
        in_specs=[sliced(inputs.shape)] * 3 + [whole(first_factor.shape), whole(second_factor.shape)],
        out_specs=sliced(packet),
        out_shape=jax.ShapeDtypeStruct(packet, BF16),
        scratch_shapes=[pltpu.VMEM((CHUNK // LANES, positions, LANES), F32)],
        compiler_params=pltpu.CompilerParams(vmem_limit_bytes=60 * MIB),
        cost_estimate=cost(2 * macs * (width_p + width_q), 6 * MIB),
        name="send",
    )(inputs, gates, cotangent, first_factor, second_factor)
    got = lax.all_to_all(send, "seq", 0, 0, tiled=True)

    lines = (blocks * width_q + rows * width_p // 2) // shares
    parts = pl.pallas_call(
        grads_kernel,
        in_specs=near(4),
        out_specs=pl.BlockSpec(memory_space=pltpu.VMEM),
        out_shape=jax.ShapeDtypeStruct((shares, lines, width_q), BF16),
        scratch_shapes=[pltpu.VMEM((channels // LANES, positions, LANES), F32)],
        compiler_params=pltpu.CompilerParams(vmem_limit_bytes=20 * MIB),
        cost_estimate=cost(2 * macs * (width_p + width_q), 6 * MIB),
        name="grads",
    )(got, inputs, gates, cotangent)
    sums = lax.all_to_all(parts, "batch", 0, 0, tiled=True)

    input_grad = pl.pallas_call(
        input_kernel,
        in_specs=near(2),
        out_specs=pl.BlockSpec(memory_space=pltpu.VMEM),
        out_shape=jax.ShapeDtypeStruct(inputs.shape, BF16),
        compiler_params=pltpu.CompilerParams(vmem_limit_bytes=20 * MIB),
        cost_estimate=cost(2 * macs * width_q, 3 * MIB),
        name="input",
    )(got, first_factor)

    first_grad, second_grad = pl.pallas_call(
        sum_kernel,
        in_specs=near(1),
        out_specs=near(2),
        out_shape=[
            jax.ShapeDtypeStruct((blocks, width_q // shares, width_q), F32),
            jax.ShapeDtypeStruct((rows, width_p // shares, width_p), F32),
        ],
        compiler_params=pltpu.CompilerParams(vmem_limit_bytes=20 * MIB),
        cost_estimate=cost(0, MIB),
        name="sums",
    )(sums)
    return input_grad, first_grad, second_grad


def solution(mesh):
    in_specs = (
        P("batch", "seq", None),
        P("batch", "seq", None),
        P("batch", "seq", None),
        P("seq", None, None),
        P("seq", None, None),
    )
    out_specs = (P("batch", "seq", None), P("seq", "batch", None), P("seq", "batch", None))
    return jax.shard_map(
        per_device, mesh=mesh, in_specs=in_specs, out_specs=out_specs, check_vma=False
    )
```

```python
import jax
import jax.numpy as jnp
from jax import lax
from jax.experimental import pallas as pl
from jax.experimental.pallas import tpu as pltpu
from jax.sharding import PartitionSpec as P

F32 = jnp.float32
BF16 = jnp.bfloat16
CHUNK = 256
LANES = 128
MIB = 1024 * 1024
LONG = 1 << 36


def dot(a, b, contract_a, contract_b):
    return lax.dot_general(a, b, (((contract_a,), (contract_b,)), ((), ())), preferred_element_type=F32)


def product(cotangent, gates):
    return (cotangent.astype(F32) * gates.astype(F32)).astype(BF16)


def send_kernel(inputs, gates, cotangent, first, second, send, spread):
    rows, width_p, _ = second.shape
    blocks, width_q, _ = first.shape
    owners, lines, _ = send.shape
    lines //= 2
    lanes = spread.shape[0] // 2
    for q in range(rows):
        part = pl.ds(q * width_p, width_p)
        back = dot(second[q], product(cotangent[0, part, :], gates[0, part, :]), 0, 0)
        for lane in range(lanes):
            spread[lane, pl.ds(q, width_p, stride=rows), :] = back[:, lane * LANES:(lane + 1) * LANES]
    for p in range(blocks):
        mixed = dot(first[p], inputs[0, p * width_q:(p + 1) * width_q, :], 1, 0)
        for lane in range(lanes):
            spread[lanes + lane, pl.ds(p, width_q, stride=blocks), :] = (
                mixed[:, lane * LANES:(lane + 1) * LANES]
            )
    for half in range(2):
        for lane in range(lanes):
            send[:, half * lines:(half + 1) * lines, lane * LANES:(lane + 1) * LANES] = (
                spread[half * lanes + lane].reshape(owners, lines, LANES).astype(BF16)
            )


def share_kernel(side, inputs, gates, cotangent, own, other, gates_in, cotangent_in, inputs_in, scaled, sems):
    half = own.shape[0] // 2
    here = pl.ds(pl.multiple_of(side[0] * half, half), half)
    there = pl.ds(pl.multiple_of((1 - side[0]) * half, half), half)
    top, bottom = pl.ds(0, half), pl.ds(half, half)
    entering = [
        pltpu.make_async_copy(inputs.at[0], inputs_in, sems.at[0]),
        pltpu.make_async_copy(gates.at[0], gates_in, sems.at[1]),
        pltpu.make_async_copy(cotangent.at[0], cotangent_in, sems.at[2]),
    ]
    leaving = [
        pltpu.make_async_copy(inputs_in.at[there], other.at[top], sems.at[3]),
        pltpu.make_async_copy(inputs_in.at[here], own.at[top], sems.at[4]),
        pltpu.make_async_copy(scaled.at[there], other.at[bottom], sems.at[5]),
        pltpu.make_async_copy(scaled.at[here], own.at[bottom], sems.at[6]),
    ]
    for copy in entering:
        copy.start()
    entering[0].wait()
    leaving[0].start()
    leaving[1].start()
    entering[1].wait()
    entering[2].wait()
    scaled[...] = product(cotangent_in[...], gates_in[...])
    leaving[2].start()
    leaving[3].start()
    for copy in leaving:
        copy.wait()


def theirs_kernel(side, after, got, theirs):
    owners, _, lines, channels = got.shape
    theirs[...] = got[:, pl.ds(1 - side[0], 1), :lines // 2, :].reshape(theirs.shape)


def grads_kernel(side, after, got, own, came, out, parts_in, spread, sems):
    owners, _, lines, channels = got.shape
    lines //= 2
    shares, height, width_q = out.shape
    width_p = LANES
    half = own.shape[0] // 2
    rows = half // width_p
    blocks = half // width_q
    depth = lines // rows
    lanes = channels // LANES
    cut = blocks * width_q // shares
    leaving = [
        pltpu.make_async_copy(parts_in.at[:, part], out.at[:, part], sems.at[n])
        for n, part in enumerate((pl.ds(0, cut), pl.ds(cut, height - cut)))
    ]
    firsts = [None] * blocks
    for away in range(2):
        packet = got[:, pl.ds(side[0] ^ away, 1), :, :].reshape(owners, 2 * lines, channels).astype(F32)
        wide = packet[:, :lines].reshape(owners, blocks, lines // blocks, channels)
        backs = [wide[:, p].reshape(width_q, channels).astype(BF16) for p in range(blocks)]
        for lane in range(lanes):
            spread[away, lane] = (
                packet[:, lines:, lane * LANES:(lane + 1) * LANES].reshape(owners * lines, LANES)
            )
        for p in range(blocks):
            source = (own, came)[away][p * width_q:(p + 1) * width_q, :]
            grad = dot(backs[p], source, 1, 1)
            firsts[p] = grad if firsts[p] is None else firsts[p] + grad
    parts_in[:, :cut, :] = jnp.concatenate(
        [grad.reshape(shares, width_q // shares, width_q) for grad in firsts], axis=1
    ).astype(BF16)
    leaving[0].start()
    seconds = []
    for q in range(rows):
        total = None
        for away in range(2):
            mixed = jnp.concatenate([
                jnp.concatenate([
                    spread[away, lane, pl.ds(q * depth + p, owners, stride=lines), :] for lane in range(lanes)
                ], axis=1)
                for p in range(depth)
            ], axis=0).astype(BF16)
            left = (own, came)[away][half + q * width_p:half + (q + 1) * width_p, :]
            grad = dot(left, mixed, 1, 1)
            total = grad if total is None else total + grad
        seconds.append(total.reshape(shares, width_p // shares, width_p))
    parts_in[:, cut:, :] = jnp.concatenate([
        jnp.concatenate([seconds[q], seconds[q + rows // 2]], axis=2) for q in range(rows // 2)
    ], axis=1).astype(BF16)
    leaving[1].start()
    leaving[0].wait()
    leaving[1].wait()


def own_kernel(side, got, factor, out, out_in, sems):
    owners, _, lines, channels = got.shape
    blocks, width, _ = factor.shape
    half = blocks // 2
    packet = got[:, pl.ds(side[0], 1), :lines // 2, :].reshape(owners, lines // 2, channels)
    half_input(packet, factor, side[0], out_in)
    there = pl.ds(pl.multiple_of(side[0] * half * width, half * width), half * width)
    copy = pltpu.make_async_copy(out_in, out.at[0, there], sems.at[0])
    copy.start()
    copy.wait()


def other_kernel(side, came, factor, grad, out, out_in, sems):
    blocks, width, _ = factor.shape
    half = blocks // 2
    half_input(came[...], factor, 1 - side[0], out_in)
    there = pl.ds(pl.multiple_of((1 - side[0]) * half * width, half * width), half * width)
    copy = pltpu.make_async_copy(out_in, out.at[0, there], sems.at[0])
    copy.start()
    copy.wait()


def half_input(packet, factor, at, out):
    owners, lines, channels = packet.shape
    blocks, width, _ = factor.shape
    half = blocks // 2
    wide = packet.astype(F32).reshape(owners, half, lines // half, channels)
    for p in range(half):
        back = wide[:, p].reshape(width, channels).astype(BF16)
        out[p * width:(p + 1) * width, :] = dot(factor[at * half + p], back, 0, 0).astype(BF16)


def sum_kernel(got, first, second):
    shares = got.shape[0]
    blocks, height, width_q = first.shape
    rows, depth, width_p = second.shape
    cut = blocks // 2 * height
    owners = width_p // blocks
    row = lax.broadcasted_iota(jnp.int32, (width_p, width_p), 0)
    column = lax.broadcasted_iota(jnp.int32, (width_p, width_p), 1)
    order = ((row % owners) * blocks + row // owners == column).astype(F32)
    for half in range(2):
        total = got[half].astype(F32)
        for share in range(2 + half, shares, 2):
            total = total + got[share].astype(F32)
        total = total * (1.0 / shares)
        at = half * blocks // 2
        first[at:at + blocks // 2] = total[:cut].reshape(blocks // 2, height, width_q)
        for side in range(2):
            lines = lax.dot_general(
                total[cut:, side * width_p:(side + 1) * width_p], order, (((1,), (0,)), ((), ())),
                precision=lax.Precision.HIGHEST, preferred_element_type=F32,
            )
            at = half * rows // 2 + side * rows // 4
            second[at:at + rows // 4] = lines.reshape(rows // 4, depth, width_p)


def whole(shape):
    return pl.BlockSpec(shape, lambda i: (0,) * len(shape))


def sliced(shape):
    return pl.BlockSpec(shape[:-1] + (CHUNK,), lambda i: (0,) * (len(shape) - 1) + (i,))


def cost(flops, bytes_accessed):
    return pl.CostEstimate(flops=flops, bytes_accessed=bytes_accessed, transcendentals=0)


def local(kernel, name, operands, out, scratch=(), sems=0, flops=0, size=3, aliases=None, close=0, scalars=0, far=0):
    space = pltpu.HBM if sems else pltpu.VMEM
    scalars = 1 if sems else scalars
    lead = [pl.BlockSpec(memory_space=pltpu.SMEM)] * scalars + [pl.BlockSpec(memory_space=pltpu.HBM)] * far
    return pl.pallas_call(
        kernel,
        in_specs=lead
        + [pl.BlockSpec(memory_space=pltpu.VMEM)] * close
        + [pl.BlockSpec(memory_space=space)] * (len(operands) - len(lead) - close),
        out_specs=[pl.BlockSpec(memory_space=space)] * len(out),
        input_output_aliases=aliases or {},
        out_shape=[jax.ShapeDtypeStruct(shape, dtype) for shape, dtype in out],
        scratch_shapes=[pltpu.VMEM(shape, dtype) for shape, dtype in scratch]
        + [pltpu.SemaphoreType.DMA((sems,))] * bool(sems),
        compiler_params=pltpu.CompilerParams(vmem_limit_bytes=24 * MIB),
        cost_estimate=cost(flops, size * MIB),
        name=name,
    )(*operands)


def per_device(inputs, gates, cotangent, first_factor, second_factor):
    _, positions, channels = inputs.shape
    blocks, width_q, _ = first_factor.shape
    rows, width_p, _ = second_factor.shape
    owners = lax.axis_size("seq")
    shares = lax.axis_size("batch")
    lines = blocks * rows
    half = positions // 2
    macs = positions * channels
    side = (lax.axis_index("batch").astype(jnp.int32) % 2).reshape(1)
    groups = [
        [owner * shares + pair * 2 + of for owner in range(owners) for of in range(2)]
        for pair in range(shares // 2)
    ]

    def swap(x):
        return lax.ppermute(x, "batch", [(i, i ^ 1) for i in range(shares)])

    packet = (owners * 2, lines, channels)
    send = pl.pallas_call(
        send_kernel,
        grid=(channels // CHUNK,),
        in_specs=[sliced(inputs.shape)] * 3 + [whole(first_factor.shape), whole(second_factor.shape)],
        out_specs=sliced(packet),
        out_shape=jax.ShapeDtypeStruct(packet, BF16),
        scratch_shapes=[pltpu.VMEM((2 * CHUNK // LANES, positions, LANES), F32)],
        compiler_params=pltpu.CompilerParams(vmem_limit_bytes=60 * MIB),
        cost_estimate=cost(2 * macs * (width_p + width_q), 6 * MIB),
        name="send",
    )(inputs, gates, cotangent, first_factor, second_factor)
    got = lax.all_to_all(send, ("seq", "batch"), 0, 0, tiled=True, axis_index_groups=groups)

    full = ((positions, channels), BF16)
    halved = ((half, channels), BF16)
    own, other = local(
        share_kernel, "share", (side, inputs, gates, cotangent), [full] * 2, [full] * 4, 7, 0, 5,
    )
    came = swap(other)

    height = (blocks * width_q + rows * width_p // 2) // 2 // shares
    got = got.reshape(owners, 2, lines, channels)
    [theirs] = local(
        theirs_kernel, "theirs", (side, came, got), [((owners, lines // 2, channels), BF16)], (), 0, 0, 1, None, 1, 1, 1,
    )
    [parts] = local(
        grads_kernel, "grads", (side, theirs, got, own, came),
        [((shares, height, width_q), BF16)],
        [((shares, height, width_q), BF16), ((2, channels // LANES, owners * lines // 2, LANES), F32)],
        2, 2 * macs * (width_p + width_q), 6, None, 3, 1, 1,
    )
    sums = lax.all_to_all(parts, "batch", 0, 0, tiled=True)
    [input_grad] = local(
        own_kernel, "own", (side, got, first_factor), [(inputs.shape, BF16)], [halved], 1, macs * width_q, 2,
        None, 2,
    )
    [input_grad] = local(
        other_kernel, "other", (side, swap(theirs), first_factor, input_grad), [(inputs.shape, BF16)], [halved],
        1, LONG, 2, {3: 0}, 2,
    )
    first_grad, second_grad = local(
        sum_kernel, "sums", (sums,),
        [
            ((blocks, width_q // shares, width_q), F32),
            ((rows, width_p // shares, width_p), F32),
        ], (), 0, 0, 1,
    )
    return input_grad, first_grad, second_grad


def solution(mesh):
    in_specs = (
        P("batch", "seq", None),
        P("batch", "seq", None),
        P("batch", "seq", None),
        P("seq", None, None),
        P("seq", None, None),
    )
    out_specs = (P("batch", "seq", None), P("seq", "batch", None), P("seq", "batch", None))
    return jax.shard_map(
        per_device, mesh=mesh, in_specs=in_specs, out_specs=out_specs, check_vma=False
    )
```

```python
import jax
import jax.numpy as jnp
from jax import lax
from jax.experimental import pallas as pl
from jax.experimental.pallas import tpu as pltpu
from jax.sharding import PartitionSpec as P

F32 = jnp.float32
BF16 = jnp.bfloat16
CHUNK = 256
LANES = 128
MIB = 1024 * 1024
LONG = 1 << 36


def dot(a, b, contract_a, contract_b):
    return lax.dot_general(a, b, (((contract_a,), (contract_b,)), ((), ())), preferred_element_type=F32)


def product(cotangent, gates):
    return (cotangent.astype(F32) * gates.astype(F32)).astype(BF16)


def send_kernel(inputs, gates, cotangent, first, second, send, spread):
    rows, width_p, _ = second.shape
    blocks, width_q, _ = first.shape
    owners, lines, _ = send.shape
    lines //= 2
    lanes = spread.shape[0] // 2
    for q in range(rows):
        part = pl.ds(q * width_p, width_p)
        back = dot(second[q], product(cotangent[0, part, :], gates[0, part, :]), 0, 0)
        for lane in range(lanes):
            spread[lane, pl.ds(q, width_p, stride=rows), :] = back[:, lane * LANES:(lane + 1) * LANES]
    for p in range(blocks):
        mixed = dot(first[p], inputs[0, p * width_q:(p + 1) * width_q, :], 1, 0)
        for lane in range(lanes):
            spread[lanes + lane, pl.ds(p, width_q, stride=blocks), :] = (
                mixed[:, lane * LANES:(lane + 1) * LANES]
            )
    for half in range(2):
        for lane in range(lanes):
            send[:, half * lines:(half + 1) * lines, lane * LANES:(lane + 1) * LANES] = (
                spread[half * lanes + lane].reshape(owners, lines, LANES).astype(BF16)
            )


def share_kernel(side, inputs, gates, cotangent, own, other, gates_in, cotangent_in, inputs_in, scaled, sems):
    half = own.shape[0] // 2
    here = pl.ds(pl.multiple_of(side[0] * half, half), half)
    there = pl.ds(pl.multiple_of((1 - side[0]) * half, half), half)
    top, bottom = pl.ds(0, half), pl.ds(half, half)
    entering = [
        pltpu.make_async_copy(inputs.at[0], inputs_in, sems.at[0]),
        pltpu.make_async_copy(gates.at[0], gates_in, sems.at[1]),
        pltpu.make_async_copy(cotangent.at[0], cotangent_in, sems.at[2]),
    ]
    leaving = [
        pltpu.make_async_copy(inputs_in.at[there], other.at[top], sems.at[3]),
        pltpu.make_async_copy(inputs_in.at[here], own.at[top], sems.at[4]),
        pltpu.make_async_copy(scaled.at[there], other.at[bottom], sems.at[5]),
        pltpu.make_async_copy(scaled.at[here], own.at[bottom], sems.at[6]),
    ]
    for copy in entering:
        copy.start()
    entering[0].wait()
    leaving[0].start()
    leaving[1].start()
    entering[1].wait()
    entering[2].wait()
    scaled[...] = product(cotangent_in[...], gates_in[...])
    leaving[2].start()
    leaving[3].start()
    for copy in leaving:
        copy.wait()


def theirs_kernel(side, after, got, theirs):
    owners, _, lines, channels = got.shape
    theirs[...] = got[:, pl.ds(1 - side[0], 1), :lines // 2, :].reshape(theirs.shape)


def grads_kernel(side, after, got, own, came, out, parts_in, spread, sems):
    owners, _, lines, channels = got.shape
    lines //= 2
    shares, height, width_q = out.shape
    width_p = LANES
    half = own.shape[0] // 2
    rows = half // width_p
    blocks = half // width_q
    depth = lines // rows
    lanes = channels // LANES
    cut = blocks * width_q // shares
    leaving = [
        pltpu.make_async_copy(parts_in.at[:, part], out.at[:, part], sems.at[n])
        for n, part in enumerate((pl.ds(0, cut), pl.ds(cut, height - cut)))
    ]
    firsts = [None] * blocks
    for away in range(2):
        packet = got[:, pl.ds(side[0] ^ away, 1), :, :].reshape(owners, 2 * lines, channels).astype(F32)
        wide = packet[:, :lines].reshape(owners, blocks, lines // blocks, channels)
        backs = [wide[:, p].reshape(width_q, channels).astype(BF16) for p in range(blocks)]
        for lane in range(lanes):
            spread[away, lane] = (
                packet[:, lines:, lane * LANES:(lane + 1) * LANES].reshape(owners * lines, LANES)
            )
        for p in range(blocks):
            source = (own, came)[away][p * width_q:(p + 1) * width_q, :]
            grad = dot(backs[p], source, 1, 1)
            firsts[p] = grad if firsts[p] is None else firsts[p] + grad
    parts_in[:, :cut, :] = jnp.concatenate(
        [grad.reshape(shares, width_q // shares, width_q) for grad in firsts], axis=1
    ).astype(BF16)
    leaving[0].start()
    seconds = []
    for q in range(rows):
        total = None
        for away in range(2):
            mixed = jnp.concatenate([
                jnp.concatenate([
                    spread[away, lane, pl.ds(q * depth + p, owners, stride=lines), :] for lane in range(lanes)
                ], axis=1)
                for p in range(depth)
            ], axis=0).astype(BF16)
            left = (own, came)[away][half + q * width_p:half + (q + 1) * width_p, :]
            grad = dot(left, mixed, 1, 1)
            total = grad if total is None else total + grad
        seconds.append(total.reshape(shares, width_p // shares, width_p))
    parts_in[:, cut:, :] = jnp.concatenate([
        jnp.concatenate([seconds[q], seconds[q + rows // 2]], axis=2) for q in range(rows // 2)
    ], axis=1).astype(BF16)
    leaving[1].start()
    leaving[0].wait()
    leaving[1].wait()


def own_kernel(side, got, factor, out, out_in, sems):
    owners, _, lines, channels = got.shape
    blocks, width, _ = factor.shape
    half = blocks // 2
    packet = got[:, pl.ds(side[0], 1), :lines // 2, :].reshape(owners, lines // 2, channels)
    half_input(packet, factor, side[0], out_in)
    there = pl.ds(pl.multiple_of(side[0] * half * width, half * width), half * width)
    copy = pltpu.make_async_copy(out_in, out.at[0, there], sems.at[0])
    copy.start()
    copy.wait()


def other_kernel(side, came, factor, grad, out, out_in, sems):
    blocks, width, _ = factor.shape
    half = blocks // 2
    half_input(came[...], factor, 1 - side[0], out_in)
    there = pl.ds(pl.multiple_of((1 - side[0]) * half * width, half * width), half * width)
    copy = pltpu.make_async_copy(out_in, out.at[0, there], sems.at[0])
    copy.start()
    copy.wait()


def half_input(packet, factor, at, out):
    owners, lines, channels = packet.shape
    blocks, width, _ = factor.shape
    half = blocks // 2
    wide = packet.astype(F32).reshape(owners, half, lines // half, channels)
    for p in range(half):
        back = wide[:, p].reshape(width, channels).astype(BF16)
        out[p * width:(p + 1) * width, :] = dot(factor[at * half + p], back, 0, 0).astype(BF16)


def sum_kernel(got, first, second):
    shares = got.shape[0]
    blocks, height, width_q = first.shape
    rows, depth, width_p = second.shape
    cut = blocks // 2 * height
    owners = width_p // blocks
    row = lax.broadcasted_iota(jnp.int32, (width_p, width_p), 0)
    column = lax.broadcasted_iota(jnp.int32, (width_p, width_p), 1)
    order = ((row % owners) * blocks + row // owners == column).astype(F32)
    for half in range(2):
        total = got[half].astype(F32)
        for share in range(2 + half, shares, 2):
            total = total + got[share].astype(F32)
        total = total * (1.0 / shares)
        at = half * blocks // 2
        first[at:at + blocks // 2] = total[:cut].reshape(blocks // 2, height, width_q)
        for side in range(2):
            lines = lax.dot_general(
                total[cut:, side * width_p:(side + 1) * width_p], order, (((1,), (0,)), ((), ())),
                precision=lax.Precision.HIGHEST, preferred_element_type=F32,
            )
            at = half * rows // 2 + side * rows // 4
            second[at:at + rows // 4] = lines.reshape(rows // 4, depth, width_p)


def whole(shape):
    return pl.BlockSpec(shape, lambda i: (0,) * len(shape))


def sliced(shape):
    return pl.BlockSpec(shape[:-1] + (CHUNK,), lambda i: (0,) * (len(shape) - 1) + (i,))


def cost(flops, bytes_accessed):
    return pl.CostEstimate(flops=flops, bytes_accessed=bytes_accessed, transcendentals=0)


def local(kernel, name, operands, out, scratch=(), sems=0, flops=0, size=3, aliases=None, close=0, scalars=0, far=0, limit=24 * MIB):
    space = pltpu.HBM if sems else pltpu.VMEM
    scalars = 1 if sems else scalars
    lead = [pl.BlockSpec(memory_space=pltpu.SMEM)] * scalars + [pl.BlockSpec(memory_space=pltpu.HBM)] * far
    return pl.pallas_call(
        kernel,
        in_specs=lead
        + [pl.BlockSpec(memory_space=pltpu.VMEM)] * close
        + [pl.BlockSpec(memory_space=space)] * (len(operands) - len(lead) - close),
        out_specs=[pl.BlockSpec(memory_space=space)] * len(out),
        input_output_aliases=aliases or {},
        out_shape=[jax.ShapeDtypeStruct(shape, dtype) for shape, dtype in out],
        scratch_shapes=[pltpu.VMEM(shape, dtype) for shape, dtype in scratch]
        + [pltpu.SemaphoreType.DMA((sems,))] * bool(sems),
        compiler_params=pltpu.CompilerParams(vmem_limit_bytes=limit),
        cost_estimate=cost(flops, size * MIB),
        name=name,
    )(*operands)


def per_device(inputs, gates, cotangent, first_factor, second_factor):
    _, positions, channels = inputs.shape
    blocks, width_q, _ = first_factor.shape
    rows, width_p, _ = second_factor.shape
    owners = lax.axis_size("seq")
    shares = lax.axis_size("batch")
    lines = blocks * rows
    half = positions // 2
    macs = positions * channels
    side = (lax.axis_index("batch").astype(jnp.int32) % 2).reshape(1)
    groups = [
        [owner * shares + pair * 2 + of for owner in range(owners) for of in range(2)]
        for pair in range(shares // 2)
    ]

    def swap(x):
        return lax.ppermute(x, "batch", [(i, i ^ 1) for i in range(shares)])

    packet = (owners * 2, lines, channels)
    send = pl.pallas_call(
        send_kernel,
        grid=(channels // CHUNK,),
        in_specs=[sliced(inputs.shape)] * 3 + [whole(first_factor.shape), whole(second_factor.shape)],
        out_specs=sliced(packet),
        out_shape=jax.ShapeDtypeStruct(packet, BF16),
        scratch_shapes=[pltpu.VMEM((2 * CHUNK // LANES, positions, LANES), F32)],
        compiler_params=pltpu.CompilerParams(vmem_limit_bytes=60 * MIB),
        cost_estimate=cost(2 * macs * (width_p + width_q), 6 * MIB),
        name="send",
    )(inputs, gates, cotangent, first_factor, second_factor)
    got = lax.all_to_all(send, ("seq", "batch"), 0, 0, tiled=True, axis_index_groups=groups)

    full = ((positions, channels), BF16)
    halved = ((half, channels), BF16)
    own, other = local(
        share_kernel, "share", (side, inputs, gates, cotangent), [full] * 2, [full] * 4, 7, 0, 5, limit=60 * MIB,
    )
    came = swap(other)

    height = (blocks * width_q + rows * width_p // 2) // 2 // shares
    got = got.reshape(owners, 2, lines, channels)
    [theirs] = local(
        theirs_kernel, "theirs", (side, came, got), [((owners, lines // 2, channels), BF16)], (), 0, 0, 1, None, 1, 1, 1,
    )
    [parts] = local(
        grads_kernel, "grads", (side, theirs, got, own, came),
        [((shares, height, width_q), BF16)],
        [((shares, height, width_q), BF16), ((2, channels // LANES, owners * lines // 2, LANES), F32)],
        2, 2 * macs * (width_p + width_q), 6, None, 3, 1, 1,
    )
    sums = lax.all_to_all(parts, "batch", 0, 0, tiled=True)
    [input_grad] = local(
        own_kernel, "own", (side, got, first_factor), [(inputs.shape, BF16)], [halved], 1, macs * width_q, 2,
        None, 2,
    )
    [input_grad] = local(
        other_kernel, "other", (side, swap(theirs), first_factor, input_grad), [(inputs.shape, BF16)], [halved],
        1, LONG, 2, {3: 0}, 2,
    )
    first_grad, second_grad = local(
        sum_kernel, "sums", (sums,),
        [
            ((blocks, width_q // shares, width_q), F32),
            ((rows, width_p // shares, width_p), F32),
        ], (), 0, 0, 1,
    )
    return input_grad, first_grad, second_grad


def solution(mesh):
    in_specs = (
        P("batch", "seq", None),
        P("batch", "seq", None),
        P("batch", "seq", None),
        P("seq", None, None),
        P("seq", None, None),
    )
    out_specs = (P("batch", "seq", None), P("seq", "batch", None), P("seq", "batch", None))
    return jax.shard_map(
        per_device, mesh=mesh, in_specs=in_specs, out_specs=out_specs, check_vma=False
    )
```

```python
import jax
import jax.numpy as jnp
from jax import lax
from jax.experimental import pallas as pl
from jax.experimental.pallas import tpu as pltpu
from jax.sharding import PartitionSpec as P

F32 = jnp.float32
BF16 = jnp.bfloat16
CHUNK = 256
LANES = 128
MIB = 1024 * 1024
LONG = 1 << 36


def dot(a, b, contract_a, contract_b):
    return lax.dot_general(a, b, (((contract_a,), (contract_b,)), ((), ())), preferred_element_type=F32)


def product(cotangent, gates):
    return (cotangent.astype(F32) * gates.astype(F32)).astype(BF16)


def send_kernel(inputs, gates, cotangent, first, second, send, spread):
    rows, width_p, _ = second.shape
    blocks, width_q, _ = first.shape
    owners, lines, _ = send.shape
    lines //= 2
    lanes = spread.shape[0] // 2
    for q in range(rows):
        part = pl.ds(q * width_p, width_p)
        back = dot(second[q], product(cotangent[0, part, :], gates[0, part, :]), 0, 0)
        for lane in range(lanes):
            spread[lane, pl.ds(q, width_p, stride=rows), :] = back[:, lane * LANES:(lane + 1) * LANES]
    for p in range(blocks):
        mixed = dot(first[p], inputs[0, p * width_q:(p + 1) * width_q, :], 1, 0)
        for lane in range(lanes):
            spread[lanes + lane, pl.ds(p, width_q, stride=blocks), :] = (
                mixed[:, lane * LANES:(lane + 1) * LANES]
            )
    for half in range(2):
        for lane in range(lanes):
            send[:, half * lines:(half + 1) * lines, lane * LANES:(lane + 1) * LANES] = (
                spread[half * lanes + lane].reshape(owners, lines, LANES).astype(BF16)
            )


def share_kernel(side, inputs, gates, cotangent, own, other, gates_in, cotangent_in, inputs_in, scaled, sems):
    half = own.shape[0] // 2
    here = pl.ds(pl.multiple_of(side[0] * half, half), half)
    there = pl.ds(pl.multiple_of((1 - side[0]) * half, half), half)
    top, bottom = pl.ds(0, half), pl.ds(half, half)
    entering = [
        pltpu.make_async_copy(inputs.at[0], inputs_in, sems.at[0]),
        pltpu.make_async_copy(gates.at[0], gates_in, sems.at[1]),
        pltpu.make_async_copy(cotangent.at[0], cotangent_in, sems.at[2]),
    ]
    leaving = [
        pltpu.make_async_copy(inputs_in.at[there], other.at[top], sems.at[3]),
        pltpu.make_async_copy(inputs_in.at[here], own.at[top], sems.at[4]),
        pltpu.make_async_copy(scaled.at[there], other.at[bottom], sems.at[5]),
        pltpu.make_async_copy(scaled.at[here], own.at[bottom], sems.at[6]),
    ]
    for copy in entering:
        copy.start()
    entering[0].wait()
    leaving[0].start()
    leaving[1].start()
    entering[1].wait()
    entering[2].wait()
    scaled[...] = product(cotangent_in[...], gates_in[...])
    leaving[2].start()
    leaving[3].start()
    for copy in leaving:
        copy.wait()


def theirs_kernel(side, after, got, theirs):
    owners, _, lines, channels = got.shape
    theirs[...] = got[:, pl.ds(1 - side[0], 1), :lines // 2, :].reshape(theirs.shape)


def grads_kernel(side, after, got, own, came, out, mine, parts_in, spread, sems):
    owners, _, lines, channels = got.shape
    lines //= 2
    shares, height, width_q = out.shape
    width_p = LANES
    half = own.shape[0] // 2
    rows = half // width_p
    blocks = half // width_q
    depth = lines // rows
    lanes = channels // LANES
    cut = blocks * width_q // shares
    leaving = [
        pltpu.make_async_copy(parts_in.at[:, part], out.at[:, part], sems.at[n])
        for n, part in enumerate((pl.ds(0, cut), pl.ds(cut, height - cut)))
    ]
    leaving.append(pltpu.make_async_copy(got.at[:, side[0], pl.ds(0, lines)], mine, sems.at[2]))
    leaving[2].start()
    firsts = [None] * blocks
    for away in range(2):
        packet = got[:, pl.ds(side[0] ^ away, 1), :, :].reshape(owners, 2 * lines, channels).astype(F32)
        wide = packet[:, :lines].reshape(owners, blocks, lines // blocks, channels)
        backs = [wide[:, p].reshape(width_q, channels).astype(BF16) for p in range(blocks)]
        for lane in range(lanes):
            spread[away, lane] = (
                packet[:, lines:, lane * LANES:(lane + 1) * LANES].reshape(owners * lines, LANES)
            )
        for p in range(blocks):
            source = (own, came)[away][p * width_q:(p + 1) * width_q, :]
            grad = dot(backs[p], source, 1, 1)
            firsts[p] = grad if firsts[p] is None else firsts[p] + grad
    parts_in[:, :cut, :] = jnp.concatenate(
        [grad.reshape(shares, width_q // shares, width_q) for grad in firsts], axis=1
    ).astype(BF16)
    leaving[0].start()
    seconds = []
    for q in range(rows):
        total = None
        for away in range(2):
            mixed = jnp.concatenate([
                jnp.concatenate([
                    spread[away, lane, pl.ds(q * depth + p, owners, stride=lines), :] for lane in range(lanes)
                ], axis=1)
                for p in range(depth)
            ], axis=0).astype(BF16)
            left = (own, came)[away][half + q * width_p:half + (q + 1) * width_p, :]
            grad = dot(left, mixed, 1, 1)
            total = grad if total is None else total + grad
        seconds.append(total.reshape(shares, width_p // shares, width_p))
    parts_in[:, cut:, :] = jnp.concatenate([
        jnp.concatenate([seconds[q], seconds[q + rows // 2]], axis=2) for q in range(rows // 2)
    ], axis=1).astype(BF16)
    leaving[1].start()
    for copy in leaving:
        copy.wait()


def own_kernel(side, kept, factor, out, out_in, sems):
    blocks, width, _ = factor.shape
    half = blocks // 2
    half_input(kept[...], factor, side[0], out_in)
    there = pl.ds(pl.multiple_of(side[0] * half * width, half * width), half * width)
    copy = pltpu.make_async_copy(out_in, out.at[0, there], sems.at[0])
    copy.start()
    copy.wait()


def other_kernel(side, came, factor, grad, out, out_in, sems):
    blocks, width, _ = factor.shape
    half = blocks // 2
    half_input(came[...], factor, 1 - side[0], out_in)
    there = pl.ds(pl.multiple_of((1 - side[0]) * half * width, half * width), half * width)
    copy = pltpu.make_async_copy(out_in, out.at[0, there], sems.at[0])
    copy.start()
    copy.wait()


def half_input(packet, factor, at, out):
    owners, lines, channels = packet.shape
    blocks, width, _ = factor.shape
    half = blocks // 2
    wide = packet.astype(F32).reshape(owners, half, lines // half, channels)
    for p in range(half):
        back = wide[:, p].reshape(width, channels).astype(BF16)
        out[p * width:(p + 1) * width, :] = dot(factor[at * half + p], back, 0, 0).astype(BF16)


def sum_kernel(got, first, second):
    shares = got.shape[0]
    blocks, height, width_q = first.shape
    rows, depth, width_p = second.shape
    cut = blocks // 2 * height
    owners = width_p // blocks
    row = lax.broadcasted_iota(jnp.int32, (width_p, width_p), 0)
    column = lax.broadcasted_iota(jnp.int32, (width_p, width_p), 1)
    order = ((row % owners) * blocks + row // owners == column).astype(F32)
    for half in range(2):
        total = got[half].astype(F32)
        for share in range(2 + half, shares, 2):
            total = total + got[share].astype(F32)
        total = total * (1.0 / shares)
        at = half * blocks // 2
        first[at:at + blocks // 2] = total[:cut].reshape(blocks // 2, height, width_q)
        for side in range(2):
            lines = lax.dot_general(
                total[cut:, side * width_p:(side + 1) * width_p], order, (((1,), (0,)), ((), ())),
                precision=lax.Precision.HIGHEST, preferred_element_type=F32,
            )
            at = half * rows // 2 + side * rows // 4
            second[at:at + rows // 4] = lines.reshape(rows // 4, depth, width_p)


def whole(shape):
    return pl.BlockSpec(shape, lambda i: (0,) * len(shape))


def sliced(shape):
    return pl.BlockSpec(shape[:-1] + (CHUNK,), lambda i: (0,) * (len(shape) - 1) + (i,))


def cost(flops, bytes_accessed):
    return pl.CostEstimate(flops=flops, bytes_accessed=bytes_accessed, transcendentals=0)


def local(kernel, name, operands, out, scratch=(), sems=0, flops=0, size=3, aliases=None, close=0, scalars=0, far=0, limit=24 * MIB):
    space = pltpu.HBM if sems else pltpu.VMEM
    scalars = 1 if sems else scalars
    lead = [pl.BlockSpec(memory_space=pltpu.SMEM)] * scalars + [pl.BlockSpec(memory_space=pltpu.HBM)] * far
    return pl.pallas_call(
        kernel,
        in_specs=lead
        + [pl.BlockSpec(memory_space=pltpu.VMEM)] * close
        + [pl.BlockSpec(memory_space=space)] * (len(operands) - len(lead) - close),
        out_specs=[pl.BlockSpec(memory_space=space)] * len(out),
        input_output_aliases=aliases or {},
        out_shape=[jax.ShapeDtypeStruct(shape, dtype) for shape, dtype in out],
        scratch_shapes=[pltpu.VMEM(shape, dtype) for shape, dtype in scratch]
        + [pltpu.SemaphoreType.DMA((sems,))] * bool(sems),
        compiler_params=pltpu.CompilerParams(vmem_limit_bytes=limit),
        cost_estimate=cost(flops, size * MIB),
        name=name,
    )(*operands)


def per_device(inputs, gates, cotangent, first_factor, second_factor):
    _, positions, channels = inputs.shape
    blocks, width_q, _ = first_factor.shape
    rows, width_p, _ = second_factor.shape
    owners = lax.axis_size("seq")
    shares = lax.axis_size("batch")
    lines = blocks * rows
    half = positions // 2
    macs = positions * channels
    side = (lax.axis_index("batch").astype(jnp.int32) % 2).reshape(1)
    groups = [
        [owner * shares + pair * 2 + of for owner in range(owners) for of in range(2)]
        for pair in range(shares // 2)
    ]

    def swap(x):
        return lax.ppermute(x, "batch", [(i, i ^ 1) for i in range(shares)])

    packet = (owners * 2, lines, channels)
    send = pl.pallas_call(
        send_kernel,
        grid=(channels // CHUNK,),
        in_specs=[sliced(inputs.shape)] * 3 + [whole(first_factor.shape), whole(second_factor.shape)],
        out_specs=sliced(packet),
        out_shape=jax.ShapeDtypeStruct(packet, BF16),
        scratch_shapes=[pltpu.VMEM((2 * CHUNK // LANES, positions, LANES), F32)],
        compiler_params=pltpu.CompilerParams(vmem_limit_bytes=60 * MIB),
        cost_estimate=cost(2 * macs * (width_p + width_q), 6 * MIB),
        name="send",
    )(inputs, gates, cotangent, first_factor, second_factor)
    got = lax.all_to_all(send, ("seq", "batch"), 0, 0, tiled=True, axis_index_groups=groups)

    full = ((positions, channels), BF16)
    halved = ((half, channels), BF16)
    own, other = local(
        share_kernel, "share", (side, inputs, gates, cotangent), [full] * 2, [full] * 4, 7, 0, 5, limit=60 * MIB,
    )
    came = swap(other)

    height = (blocks * width_q + rows * width_p // 2) // 2 // shares
    got = got.reshape(owners, 2, lines, channels)
    [theirs] = local(
        theirs_kernel, "theirs", (side, came, got), [((owners, lines // 2, channels), BF16)], (), 0, 0, 1, None, 1, 1, 1,
    )
    parts, kept = local(
        grads_kernel, "grads", (side, theirs, got, own, came),
        [((shares, height, width_q), BF16), ((owners, lines // 2, channels), BF16)],
        [((shares, height, width_q), BF16), ((2, channels // LANES, owners * lines // 2, LANES), F32)],
        3, 2 * macs * (width_p + width_q), 6, None, 3, 1, 1,
    )
    sums = lax.all_to_all(parts, "batch", 0, 0, tiled=True)
    [input_grad] = local(
        own_kernel, "own", (side, kept, first_factor), [(inputs.shape, BF16)], [halved], 1, macs * width_q, 2,
        None, 2,
    )
    [input_grad] = local(
        other_kernel, "other", (side, swap(theirs), first_factor, input_grad), [(inputs.shape, BF16)], [halved],
        1, LONG, 2, {3: 0}, 2,
    )
    first_grad, second_grad = local(
        sum_kernel, "sums", (sums,),
        [
            ((blocks, width_q // shares, width_q), F32),
            ((rows, width_p // shares, width_p), F32),
        ], (), 0, 0, 1,
    )
    return input_grad, first_grad, second_grad


def solution(mesh):
    in_specs = (
        P("batch", "seq", None),
        P("batch", "seq", None),
        P("batch", "seq", None),
        P("seq", None, None),
        P("seq", None, None),
    )
    out_specs = (P("batch", "seq", None), P("seq", "batch", None), P("seq", "batch", None))
    return jax.shard_map(
        per_device, mesh=mesh, in_specs=in_specs, out_specs=out_specs, check_vma=False
    )
```

```python
import jax
import jax.numpy as jnp
from jax import lax
from jax.experimental import pallas as pl
from jax.experimental.pallas import tpu as pltpu
from jax.sharding import PartitionSpec as P

F32 = jnp.float32
BF16 = jnp.bfloat16
CHUNK = 256
LANES = 128
MIB = 1024 * 1024
LONG = 1 << 36


def dot(a, b, contract_a, contract_b):
    return lax.dot_general(a, b, (((contract_a,), (contract_b,)), ((), ())), preferred_element_type=F32)


def product(cotangent, gates):
    return (cotangent.astype(F32) * gates.astype(F32)).astype(BF16)


def send_kernel(inputs, gates, cotangent, first, second, send, spread):
    rows, width_p, _ = second.shape
    blocks, width_q, _ = first.shape
    owners, lines, _ = send.shape
    lines //= 2
    lanes = spread.shape[0] // 2
    for q in range(rows):
        part = pl.ds(q * width_p, width_p)
        back = dot(second[q], product(cotangent[0, part, :], gates[0, part, :]), 0, 0)
        for lane in range(lanes):
            spread[lane, pl.ds(q, width_p, stride=rows), :] = back[:, lane * LANES:(lane + 1) * LANES]
    for p in range(blocks):
        mixed = dot(first[p], inputs[0, p * width_q:(p + 1) * width_q, :], 1, 0)
        for lane in range(lanes):
            spread[lanes + lane, pl.ds(p, width_q, stride=blocks), :] = (
                mixed[:, lane * LANES:(lane + 1) * LANES]
            )
    for half in range(2):
        for lane in range(lanes):
            send[:, half * lines:(half + 1) * lines, lane * LANES:(lane + 1) * LANES] = (
                spread[half * lanes + lane].reshape(owners, lines, LANES).astype(BF16)
            )


def share_kernel(side, inputs, gates, cotangent, own, other, gates_in, cotangent_in, inputs_in, scaled, sems):
    half = own.shape[0] // 2
    here = pl.ds(pl.multiple_of(side[0] * half, half), half)
    there = pl.ds(pl.multiple_of((1 - side[0]) * half, half), half)
    top, bottom = pl.ds(0, half), pl.ds(half, half)
    entering = [
        pltpu.make_async_copy(inputs.at[0], inputs_in, sems.at[0]),
        pltpu.make_async_copy(gates.at[0], gates_in, sems.at[1]),
        pltpu.make_async_copy(cotangent.at[0], cotangent_in, sems.at[2]),
    ]
    leaving = [
        pltpu.make_async_copy(inputs_in.at[there], other.at[top], sems.at[3]),
        pltpu.make_async_copy(inputs_in.at[here], own.at[top], sems.at[4]),
        pltpu.make_async_copy(scaled.at[there], other.at[bottom], sems.at[5]),
        pltpu.make_async_copy(scaled.at[here], own.at[bottom], sems.at[6]),
    ]
    for copy in entering:
        copy.start()
    entering[0].wait()
    leaving[0].start()
    leaving[1].start()
    entering[1].wait()
    entering[2].wait()
    scaled[...] = product(cotangent_in[...], gates_in[...])
    leaving[2].start()
    leaving[3].start()
    for copy in leaving:
        copy.wait()


def theirs_kernel(side, after, got, theirs):
    owners, _, lines, channels = got.shape
    theirs[...] = got[:, pl.ds(1 - side[0], 1), :lines // 2, :].reshape(theirs.shape)


def grads_kernel(side, after, got, own, came, out, parts_in, spread, sems):
    owners, _, lines, channels = got.shape
    lines //= 2
    shares, height, width_q = out.shape
    width_p = LANES
    half = own.shape[0] // 2
    rows = half // width_p
    blocks = half // width_q
    depth = lines // rows
    lanes = channels // LANES
    cut = blocks * width_q // shares
    leaving = [
        pltpu.make_async_copy(parts_in.at[:, part], out.at[:, part], sems.at[n])
        for n, part in enumerate((pl.ds(0, cut), pl.ds(cut, height - cut)))
    ]
    firsts = [None] * blocks
    for away in range(2):
        packet = got[:, pl.ds(side[0] ^ away, 1), :, :].reshape(owners, 2 * lines, channels).astype(F32)
        wide = packet[:, :lines].reshape(owners, blocks, lines // blocks, channels)
        backs = [wide[:, p].reshape(width_q, channels).astype(BF16) for p in range(blocks)]
        for lane in range(lanes):
            spread[away, lane] = (
                packet[:, lines:, lane * LANES:(lane + 1) * LANES].reshape(owners * lines, LANES)
            )
        for p in range(blocks):
            source = (own, came)[away][p * width_q:(p + 1) * width_q, :]
            grad = dot(backs[p], source, 1, 1)
            firsts[p] = grad if firsts[p] is None else firsts[p] + grad
    parts_in[:, :cut, :] = jnp.concatenate(
        [grad.reshape(shares, width_q // shares, width_q) for grad in firsts], axis=1
    ).astype(BF16)
    leaving[0].start()
    seconds = []
    for q in range(rows):
        total = None
        for away in range(2):
            mixed = jnp.concatenate([
                jnp.concatenate([
                    spread[away, lane, pl.ds(q * depth + p, owners, stride=lines), :] for lane in range(lanes)
                ], axis=1)
                for p in range(depth)
            ], axis=0).astype(BF16)
            left = (own, came)[away][half + q * width_p:half + (q + 1) * width_p, :]
            grad = dot(left, mixed, 1, 1)
            total = grad if total is None else total + grad
        seconds.append(total.reshape(shares, width_p // shares, width_p))
    parts_in[:, cut:, :] = jnp.concatenate([
        jnp.concatenate([seconds[q], seconds[q + rows // 2]], axis=2) for q in range(rows // 2)
    ], axis=1).astype(BF16)
    leaving[1].start()
    leaving[0].wait()
    leaving[1].wait()


def own_kernel(side, got, factor, out, out_in, sems):
    owners, _, lines, channels = got.shape
    blocks, width, _ = factor.shape
    half = blocks // 2
    packet = got[:, pl.ds(side[0], 1), :lines // 2, :].reshape(owners, lines // 2, channels)
    half_input(packet, factor, side[0], out_in)
    there = pl.ds(pl.multiple_of(side[0] * half * width, half * width), half * width)
    copy = pltpu.make_async_copy(out_in, out.at[0, there], sems.at[0])
    copy.start()
    copy.wait()


def other_kernel(side, came, factor, grad, out, out_in, sems):
    blocks, width, _ = factor.shape
    half = blocks // 2
    half_input(came[...], factor, 1 - side[0], out_in)
    there = pl.ds(pl.multiple_of((1 - side[0]) * half * width, half * width), half * width)
    copy = pltpu.make_async_copy(out_in, out.at[0, there], sems.at[0])
    copy.start()
    copy.wait()


def half_input(packet, factor, at, out):
    owners, lines, channels = packet.shape
    blocks, width, _ = factor.shape
    half = blocks // 2
    wide = packet.astype(F32).reshape(owners, half, lines // half, channels)
    for p in range(half):
        back = wide[:, p].reshape(width, channels).astype(BF16)
        out[p * width:(p + 1) * width, :] = dot(factor[at * half + p], back, 0, 0).astype(BF16)


def sum_kernel(got, first, second):
    shares = got.shape[0]
    blocks, height, width_q = first.shape
    rows, depth, width_p = second.shape
    cut = blocks // 2 * height
    owners = width_p // blocks
    row = lax.broadcasted_iota(jnp.int32, (width_p, width_p), 0)
    column = lax.broadcasted_iota(jnp.int32, (width_p, width_p), 1)
    order = ((row % owners) * blocks + row // owners == column).astype(F32)
    lines = []
    for half in range(2):
        total = got[half].astype(F32)
        for share in range(2 + half, shares, 2):
            total = total + got[share].astype(F32)
        total = total * (1.0 / shares)
        at = half * blocks // 2
        first[at:at + blocks // 2] = total[:cut].reshape(blocks // 2, height, width_q)
        lines += [total[cut:, :width_p], total[cut:, width_p:]]
    second[...] = lax.dot_general(
        jnp.concatenate(lines, axis=0), order, (((1,), (0,)), ((), ())),
        precision=lax.Precision.HIGHEST, preferred_element_type=F32,
    ).reshape(second.shape)


def whole(shape):
    return pl.BlockSpec(shape, lambda i: (0,) * len(shape))


def sliced(shape):
    return pl.BlockSpec(shape[:-1] + (CHUNK,), lambda i: (0,) * (len(shape) - 1) + (i,))


def cost(flops, bytes_accessed):
    return pl.CostEstimate(flops=flops, bytes_accessed=bytes_accessed, transcendentals=0)


def local(kernel, name, operands, out, scratch=(), sems=0, flops=0, size=3, aliases=None, close=0, scalars=0, far=0, limit=24 * MIB):
    space = pltpu.HBM if sems else pltpu.VMEM
    scalars = 1 if sems else scalars
    lead = [pl.BlockSpec(memory_space=pltpu.SMEM)] * scalars + [pl.BlockSpec(memory_space=pltpu.HBM)] * far
    return pl.pallas_call(
        kernel,
        in_specs=lead
        + [pl.BlockSpec(memory_space=pltpu.VMEM)] * close
        + [pl.BlockSpec(memory_space=space)] * (len(operands) - len(lead) - close),
        out_specs=[pl.BlockSpec(memory_space=space)] * len(out),
        input_output_aliases=aliases or {},
        out_shape=[jax.ShapeDtypeStruct(shape, dtype) for shape, dtype in out],
        scratch_shapes=[pltpu.VMEM(shape, dtype) for shape, dtype in scratch]
        + [pltpu.SemaphoreType.DMA((sems,))] * bool(sems),
        compiler_params=pltpu.CompilerParams(vmem_limit_bytes=limit),
        cost_estimate=cost(flops, size * MIB),
        name=name,
    )(*operands)


def per_device(inputs, gates, cotangent, first_factor, second_factor):
    _, positions, channels = inputs.shape
    blocks, width_q, _ = first_factor.shape
    rows, width_p, _ = second_factor.shape
    owners = lax.axis_size("seq")
    shares = lax.axis_size("batch")
    lines = blocks * rows
    half = positions // 2
    macs = positions * channels
    side = (lax.axis_index("batch").astype(jnp.int32) % 2).reshape(1)
    groups = [
        [owner * shares + pair * 2 + of for owner in range(owners) for of in range(2)]
        for pair in range(shares // 2)
    ]

    def swap(x):
        return lax.ppermute(x, "batch", [(i, i ^ 1) for i in range(shares)])

    packet = (owners * 2, lines, channels)
    send = pl.pallas_call(
        send_kernel,
        grid=(channels // CHUNK,),
        in_specs=[sliced(inputs.shape)] * 3 + [whole(first_factor.shape), whole(second_factor.shape)],
        out_specs=sliced(packet),
        out_shape=jax.ShapeDtypeStruct(packet, BF16),
        scratch_shapes=[pltpu.VMEM((2 * CHUNK // LANES, positions, LANES), F32)],
        compiler_params=pltpu.CompilerParams(vmem_limit_bytes=60 * MIB),
        cost_estimate=cost(2 * macs * (width_p + width_q), 6 * MIB),
        name="send",
    )(inputs, gates, cotangent, first_factor, second_factor)
    got = lax.all_to_all(send, ("seq", "batch"), 0, 0, tiled=True, axis_index_groups=groups)

    full = ((positions, channels), BF16)
    halved = ((half, channels), BF16)
    own, other = local(
        share_kernel, "share", (side, inputs, gates, cotangent), [full] * 2, [full] * 4, 7, 0, 5, limit=60 * MIB,
    )
    came = swap(other)

    height = (blocks * width_q + rows * width_p // 2) // 2 // shares
    got = got.reshape(owners, 2, lines, channels)
    [theirs] = local(
        theirs_kernel, "theirs", (side, came, got), [((owners, lines // 2, channels), BF16)], (), 0, 0, 1, None, 1, 1, 1,
    )
    [parts] = local(
        grads_kernel, "grads", (side, theirs, got, own, came),
        [((shares, height, width_q), BF16)],
        [((shares, height, width_q), BF16), ((2, channels // LANES, owners * lines // 2, LANES), F32)],
        2, 2 * macs * (width_p + width_q), 6, None, 3, 1, 1,
    )
    sums = lax.all_to_all(parts, "batch", 0, 0, tiled=True)
    [input_grad] = local(
        own_kernel, "own", (side, got, first_factor), [(inputs.shape, BF16)], [halved], 1, macs * width_q, 2,
        None, 2,
    )
    [input_grad] = local(
        other_kernel, "other", (side, swap(theirs), first_factor, input_grad), [(inputs.shape, BF16)], [halved],
        1, LONG, 2, {3: 0}, 2,
    )
    first_grad, second_grad = local(
        sum_kernel, "sums", (sums,),
        [
            ((blocks, width_q // shares, width_q), F32),
            ((rows, width_p // shares, width_p), F32),
        ], (), 0, 0, 1,
    )
    return input_grad, first_grad, second_grad


def solution(mesh):
    in_specs = (
        P("batch", "seq", None),
        P("batch", "seq", None),
        P("batch", "seq", None),
        P("seq", None, None),
        P("seq", None, None),
    )
    out_specs = (P("batch", "seq", None), P("seq", "batch", None), P("seq", "batch", None))
    return jax.shard_map(
        per_device, mesh=mesh, in_specs=in_specs, out_specs=out_specs, check_vma=False
    )
```
